32 devices in a mesh: dp: 2 (over x), tensor: 16 (over z, y, core).
Axes of the slice: x: 2, y: 2, z: 4, core: 2. Of those that a mesh axis runs over, the one named last changes fastest.
Arguments:
- grad_out: bfloat16 [512, 16384], P('tensor', 'dp'), may hold values from -6 to 6
- hidden: bfloat16 [512, 26624], P('dp', 'tensor'), may hold values from -0.25 to 0.25
- down_weight: bfloat16 [26624, 16384], P('tensor', 'dp'), may hold values from -0.046875 to 0.046875
Outputs:
- grad_hidden: bfloat16 [512, 26624], P('dp', 'tensor')
- grad_weight: bfloat16 [26624, 16384], P('tensor', 'dp')
The draws below stay inside these ranges and needn't reach their ends.
All inputs are finite; a program needn't handle non-finite values.
Results may differ from the reference program's by a relative error of at most 0.0052.
Values may be sent and summed in bfloat16 or wider, within the bound.
A program may use at most 192 MiB of HBM per device.

```python
import jax
import jax.numpy as jnp
from jax import lax

D = 16384
FF = 26624
TOKENS = 512
N_DP = 2


def steps_of(stream_key, dims, cuts, least, top_value):
    loudness = 1.0
    for position, shards_of in cuts:
        heights = jax.random.uniform(jax.random.fold_in(jax.random.fold_in(stream_key, 6), position), (shards_of,), jnp.float32, least / len(cuts), top_value / len(cuts))
        loudness = loudness * jnp.repeat(jnp.exp(heights), dims[position] // shards_of).reshape((-1,) + (1,) * (len(dims) - 1 - position))
    return loudness


def scatter_about(own_key, extent, scale, bound, split=(), dtype=jnp.bfloat16):
    drawn = scale * jax.random.normal(own_key, extent, jnp.float32)
    if split:
        drawn = drawn * steps_of(own_key, extent, split, -0.22, 0.18)
    return jnp.clip(drawn, -bound, bound).astype(dtype)


def setup_inputs(seed: int = 0) -> dict:
    keys = jax.random.split(jax.random.key(seed), 4)
    return {
        "grad_out": scatter_about(keys[0], (TOKENS, D), 1.0, 6.0, ((0, 16), (1, 2))),
        "hidden": scatter_about(keys[1], (TOKENS, FF), TOKENS ** -0.5, 0.25, ((0, 2), (1, 16))),
        "down_weight": scatter_about(keys[2], (FF, D), D ** -0.5, 0.046875, ((0, 16), (1, 2))),
    }


def reference(grad_out, hidden, down_weight):
    col_width = D // N_DP
    running_sum = jnp.zeros((TOKENS, FF), jnp.float32)
    for group in range(N_DP):
        grad_cols = grad_out[:, group * col_width:(group + 1) * col_width]
        weight_cols = down_weight[:, group * col_width:(group + 1) * col_width]
        partial_term = lax.dot_general(grad_cols, weight_cols, (((1,), (1,)), ((), ())), preferred_element_type=jnp.float32)
        partial_term = lax.optimization_barrier(partial_term.astype(jnp.bfloat16))
        running_sum = running_sum + partial_term.astype(jnp.float32)
    grad_hidden = running_sum.astype(jnp.bfloat16)
    grad_weight = lax.dot_general(hidden, grad_out, (((0,), (0,)), ((), ())), preferred_element_type=jnp.float32)
    return grad_hidden, grad_weight.astype(jnp.bfloat16)
```

```python
import functools

import jax
import jax.numpy as jnp
from jax import lax
from jax.experimental import pallas as pl
from jax.experimental.pallas import tpu as pltpu
from jax.sharding import PartitionSpec as P

MESH = pl.DeviceIdType.MESH
Z = 4
AHEAD = 2


def tiles_of(extent, tile):
    return extent // tile, extent % tile


def gather_kernel(ny, halves, chunks, x_ref, w_ref, *refs):
    n_out = 3 if halves else 2
    g_out, part_outs = refs[0], refs[1:n_out]
    g, w, acc, part, own_sem, w_sem, g_sem, out_sem, send_sem, recv_sem = refs[n_out:]
    rows = x_ref.shape[0]
    width = g.shape[2]
    hidden_units = w.shape[1]

    me = lax.axis_index("tensor")
    core = lax.rem(me, 2)
    y = lax.rem(lax.div(me, 2), ny)
    z = lax.div(me, 2 * ny)

    def place(dz, dy, other_core=False):
        zz = lax.rem(z + dz, Z)
        yy = lax.rem(y + dy, ny)
        cc = 1 - core if other_core else core
        return (zz * ny + yy) * 2 + cc

    def block(c, who):
        return g.at[c, pl.ds(pl.multiple_of(who * rows, rows), rows), :]

    def remote(c, shard, slot, target):
        return pltpu.make_async_remote_copy(
            src_ref=block(c, shard),
            dst_ref=block(c, shard),
            send_sem=send_sem.at[c, slot],
            recv_sem=recv_sem.at[c, shard],
            device_id={"tensor": target},
            device_id_type=MESH,
        )

    def along_z(c, dz):
        return remote(c, me, dz - 1, place(dz, 0))

    def along_y(c, dz, dy):
        return remote(c, place(dz, 0), Z - 1 + dz * (ny - 1) + dy - 1, place(0, dy))

    def to_core(c, dz, dy):
        return remote(c, place(dz, dy), Z - 1 + Z * (ny - 1) + dz * ny + dy, place(0, 0, True))

    def arrived(c, shard):
        remote(c, shard, 0, place(0, 0, True)).wait_recv()

    def own(c):
        columns = pl.ds(pl.multiple_of(c * width, width), width)
        return pltpu.make_async_copy(x_ref.at[:, columns], block(c, me), own_sem.at[c])

    def weights(c):
        columns = pl.ds(pl.multiple_of(c * width, width), width)
        return pltpu.make_async_copy(w_ref.at[:, columns], w.at[c], w_sem.at[c])

    def keep(c):
        return pltpu.make_async_copy(g.at[c], g_out.at[c], g_sem.at[c])

    @pl.loop(0, chunks)
    def _(c):
        own(c).start()

    @pl.loop(0, chunks)
    def _(c):
        weights(c).start()

    barrier = pltpu.get_barrier_semaphore()
    partners = [place(dz, 0) for dz in range(1, Z)] + [place(0, dy) for dy in range(1, ny)] + [place(0, 0, True)]
    for partner in partners:
        pl.semaphore_signal(barrier, inc=1, device_id={"tensor": partner}, device_id_type=MESH)
    pl.semaphore_wait(barrier, len(partners))

    def send_own(c):
        own(c).wait()
        for dz in range(1, Z):
            along_z(c, dz).start()
        for dy in range(1, ny):
            along_y(c, 0, dy).start()
        to_core(c, 0, 0).start()

    def pass_on_z(c):
        for dz in range(1, Z):
            arrived(c, place(dz, 0))
            for dy in range(1, ny):
                along_y(c, dz, dy).start()
            to_core(c, dz, 0).start()

    def pass_on_y(c):
        for dz in range(Z):
            for dy in range(1, ny):
                arrived(c, place(dz, dy))
                to_core(c, dz, dy).start()

    def multiply(c):
        for dz in range(Z):
            for dy in range(ny):
                arrived(c, place(dz, dy, True))
        keep(c).start()
        weights(c).wait()
        full, rest = tiles_of(hidden_units, 256)

        def tile(at, size):
            acc[:, pl.ds(at, size)] += lax.dot_general(
                g[c], w[c, pl.ds(at, size), :], (((1,), (1,)), ((), ())), preferred_element_type=jnp.float32
            )

        @pl.loop(0, full)
        def _(j):
            tile(pl.multiple_of(j * 256, 256), 256)

        if rest:
            tile(full * 256, rest)

    for c in range(min(AHEAD, chunks)):
        send_own(c)
    acc[...] = jnp.zeros_like(acc)

    @pl.loop(0, chunks + 2)
    def _(i):
        @pl.when(i + AHEAD < chunks)
        def _():
            send_own(i + AHEAD)

        @pl.when(i < chunks)
        def _():
            pass_on_z(i)

        @pl.when(jnp.logical_and(i >= 1, i < chunks + 1))
        def _():
            pass_on_y(i - 1)

        @pl.when(i >= 2)
        def _():
            multiply(i - 2)

    @pl.loop(0, part.shape[0] // 64)
    def _(r):
        some = pl.ds(pl.multiple_of(r * 64, 64), 64)
        part[some, :] = acc[some, :].astype(part.dtype)

    if halves:
        half = part.shape[0] // 2
        dp = lax.axis_index("dp")
        outs = [
            pltpu.make_async_copy(
                part.at[pl.ds(pl.multiple_of(which * half, half), half), :], part_outs[n], out_sem.at[n]
            )
            for n, which in enumerate((dp, 1 - dp))
        ]
    else:
        outs = [pltpu.make_async_copy(part, part_outs[0], out_sem.at[0])]
    for out in outs:
        out.start()

    @pl.loop(0, chunks)
    def _(c):
        for dz in range(1, Z):
            along_z(c, dz).wait_send()
        for dz in range(Z):
            for dy in range(1, ny):
                along_y(c, dz, dy).wait_send()
        for dz in range(Z):
            for dy in range(ny):
                to_core(c, dz, dy).wait_send()
        keep(c).wait()

    for out in outs:
        out.wait()


def gather_and_multiply(grad_out, weight, n_dp, n_tensor):
    rows, columns = grad_out.shape
    units = weight.shape[0]
    ny = n_tensor // (2 * Z)
    width = 1024
    chunks = columns // width
    tokens = rows * n_tensor
    halves = n_dp == 2
    sends = Z - 1 + Z * (ny - 1) + Z * ny
    bf16 = jnp.bfloat16
    if halves:
        part_shapes = (jax.ShapeDtypeStruct((tokens // 2, units), bf16),) * 2
    else:
        part_shapes = (jax.ShapeDtypeStruct((tokens, units), bf16),)
    any_space = pl.BlockSpec(memory_space=pl.ANY)
    dma = pltpu.SemaphoreType.DMA
    return pl.pallas_call(
        functools.partial(gather_kernel, ny, halves, chunks),
        out_shape=(jax.ShapeDtypeStruct((chunks, tokens, width), bf16), *part_shapes),
        in_specs=[any_space] * 2,
        out_specs=(any_space,) * (1 + len(part_shapes)),
        scratch_shapes=[
            pltpu.VMEM((chunks, tokens, width), bf16),
            pltpu.VMEM((chunks, units, width), bf16),
            pltpu.VMEM((tokens, units), jnp.float32),
            pltpu.VMEM((tokens, units), bf16),
            dma((chunks,)),
            dma((chunks,)),
            dma((chunks,)),
            dma((2,)),
            dma((chunks, sends)),
            dma((chunks, n_tensor)),
        ],
        compiler_params=pltpu.CompilerParams(
            collective_id=0, has_side_effects=True, vmem_limit_bytes=56 * 1024 * 1024
        ),
        cost_estimate=pl.CostEstimate(
            flops=8 * tokens * units * columns, bytes_accessed=120 * 1024 * 1024, transcendentals=0
        ),
        name="gather_multiply",
    )(grad_out, weight)


def weight_kernel(hidden_ref, g_ref, out_ref, turned):
    @pl.when(pl.program_id(0) == 0)
    def _():
        turned[...] = hidden_ref[...].T

    size = turned.shape[0] // 2 if turned.shape[0] // 2 % 16 == 0 else turned.shape[0]

    @pl.loop(0, turned.shape[0] // size)
    def _(m):
        some = pl.ds(pl.multiple_of(m * size, size), size)
        out_ref[some, :] = jnp.dot(
            turned[some, :], g_ref[...], preferred_element_type=jnp.float32
        ).astype(out_ref.dtype)


def weight_grad_of(hidden_all, g):
    tokens, units = hidden_all.shape
    chunks, _, width = g.shape
    block = 512
    per = width // block
    return pl.pallas_call(
        weight_kernel,
        grid=(chunks * per,),
        out_shape=jax.ShapeDtypeStruct((units, chunks * width), jnp.bfloat16),
        in_specs=[
            pl.BlockSpec((tokens, units), lambda j: (0, 0)),
            pl.BlockSpec((None, tokens, block), lambda j: (j // per, 0, j % per)),
        ],
        out_specs=pl.BlockSpec((units, block), lambda j: (0, j)),
        scratch_shapes=[pltpu.VMEM((units, tokens), jnp.bfloat16)],
        compiler_params=pltpu.CompilerParams(vmem_limit_bytes=56 * 1024 * 1024),
        cost_estimate=pl.CostEstimate(
            flops=2 * tokens * units * chunks * width,
            bytes_accessed=2 * (units + tokens) * chunks * width,
            transcendentals=0,
        ),
        name="weight_grad",
    )(hidden_all, g)


def local(n_dp, n_tensor, grad_out, hidden, down_weight):
    hidden_all = lax.all_gather(hidden, "dp", axis=0, tiled=True)
    g, *parts = gather_and_multiply(grad_out, down_weight, n_dp, n_tensor)
    if n_dp == 2:
        mine, theirs = parts
        got = lax.ppermute(theirs, "dp", [(0, 1), (1, 0)])
        weight_grad = weight_grad_of(hidden_all, g)
        mine, weight_grad = lax.optimization_barrier((mine, weight_grad))
        grad_hidden = (mine.astype(jnp.float32) + got.astype(jnp.float32)).astype(jnp.bfloat16)
    else:
        grad_hidden = lax.psum_scatter(parts[0], "dp", scatter_dimension=0, tiled=True)
        weight_grad = weight_grad_of(hidden_all, g)
    return grad_hidden, weight_grad


def solution(mesh):
    return jax.shard_map(
        functools.partial(local, mesh.shape["dp"], mesh.shape["tensor"]),
        mesh=mesh,
        in_specs=(P("tensor", "dp"), P("dp", "tensor"), P("tensor", "dp")),
        out_specs=(P("dp", "tensor"), P("tensor", "dp")),
        check_vma=False,
    )
```
